32 devices in a mesh: gx: 4 (over y, x), gy: 8 (over z, core).
Axes of the slice: x: 2, y: 2, z: 4, core: 2. Of those that a mesh axis runs over, the one named last changes fastest.
Arguments:
- voxel_feats: bfloat16 [128, 64, 128], P(('gx', 'gy')), may hold values from -6 to 6
- w_first: bfloat16 [27, 128, 128], replicated, may hold values from -0.109375 to 0.109375
- w_second: bfloat16 [27, 128, 128], replicated, may hold values from -0.109375 to 0.109375
- norm_gain: float32 [2, 128], replicated, may hold values from 0.5 to 1.5
- norm_shift: float32 [2, 128], replicated, may hold values from -3 to 3
- grad_out: bfloat16 [128, 64, 128], P(('gx', 'gy')), may hold values from -6 to 6
- brick_count: int32 [32], P(('gx', 'gy')), may hold values from 1 to 4, as said below
- kernel_map: int32 [128, 27], P(('gx', 'gy')), may hold values from 0 to 12, as said below
- face_send: int32 [32, 4, 1], P(('gx', 'gy')), may hold values from 0 to 3, as said below
- corner_send: int32 [32, 4, 1], P(('gx', 'gy')), may hold values from 0 to 3, as said below
Outputs:
- out_feats: bfloat16 [128, 64, 128], P(('gx', 'gy'))
- grad_in: bfloat16 [128, 64, 128], P(('gx', 'gy'))
- weight_grads: float32 [2, 27, 128, 128], replicated
- norm_grads: float32 [4, 128], replicated
The draws below stay inside these ranges and needn't reach their ends.
Inputs may be any that keep to these rules, and one draw needn't show every extreme that they name: `brick_count`: some tile is full in every draw. `kernel_map`: direction 13 names the brick itself; index 12 is the zero brick. `face_send`: list k names bricks of the tile below its brick_count, sent to its +x, -x, +y, -y neighbour for k = 0, 1, 2, 3. `corner_send`: list k names bricks of the tile below its brick_count, sent to its (+x, +y), (+x, -y), (-x, +y), (-x, -y) neighbour for k = 0, 1, 2, 3.
All inputs are finite; a program needn't handle non-finite values.
Results may differ from the reference program's by a relative error of at most 0.006.
Values may be sent and summed in bfloat16 or wider, within the bound.
A program may use at most 128 MiB of HBM per device.

```python
import jax
import jax.numpy as jnp
from jax import lax

C = 128
NB = 4
SF = 1
SC = 1
EXT = 13
TILES = 32
BRICKS = 128
N_GX = 4
N_GY = 8


def full_tile(key):
    return jax.random.randint(jax.random.fold_in(key, 12), (), 0, TILES)


def tile_counts(key):
    drawn = jax.random.randint(jax.random.fold_in(key, 11), (TILES,), NB // 4, NB + 1)
    chosen = full_tile(key)
    return jnp.where(jnp.arange(TILES) == chosen, NB, drawn).astype(jnp.int32)


def pin_ends(lists, key):
    chosen = full_tile(key)
    tile_ids = jnp.arange(TILES)[:, None, None]
    list_ids = jnp.arange(4)[None, :, None]
    slot_ids = jnp.arange(lists.shape[2])[None, None, :]
    at_top = (tile_ids == chosen) & (list_ids == 0) & (slot_ids == 0)
    at_bottom = (tile_ids == chosen) & (list_ids == 1) & (slot_ids == 0)
    lists = jnp.where(at_top, NB - 1, lists)
    return jnp.where(at_bottom, 0, lists)


def draw_brick_count(key, part):
    return tile_counts(key)


def draw_face_send(key, part):
    counts = tile_counts(key)
    random_ints = jax.random.randint(jax.random.fold_in(key, 21), (TILES, 4, SF), 0, 1 << 20)
    return pin_ends(random_ints % counts[:, None, None], key).astype(jnp.int32)


def draw_corner_send(key, part):
    counts = tile_counts(key)
    random_ints = jax.random.randint(jax.random.fold_in(key, 22), (TILES, 4, SC), 0, 1 << 20)
    return pin_ends(random_ints % counts[:, None, None], key).astype(jnp.int32)


def draw_kernel_map(key, part):
    picked = jax.random.randint(jax.random.fold_in(key, 31), (BRICKS, 27), 0, EXT - 1)
    dropped = jax.random.randint(jax.random.fold_in(key, 32), (BRICKS, 27), 0, 10) < 3
    picked = jnp.where(dropped, EXT - 1, picked)
    itself = (jnp.arange(BRICKS) % NB)[:, None]
    center = jnp.arange(27)[None, :] == 13
    return jnp.where(center, itself, picked).astype(jnp.int32)


def block_levels(rng, shape, split, smallest, high):
    def one(axis_at, blocks):
        draws = jax.random.uniform(jax.random.fold_in(jax.random.fold_in(rng, 6), axis_at), (blocks,), jnp.float32, smallest / len(split), high / len(split))
        return jnp.repeat(jnp.exp(draws), shape[axis_at] // blocks).reshape((-1,) + (1,) * (len(shape) - axis_at - 1))

    loudness = one(*split[0])
    for cut in split[1:]:
        loudness = loudness * one(*cut)
    return loudness


def noise(stream_key, dims, scale, bound, cuts=(), held_as=jnp.bfloat16):
    level = block_levels(stream_key, dims, cuts, -0.22, 0.18) if cuts else 1.0
    entries = jax.random.normal(stream_key, dims, jnp.float32) * scale * level
    return jnp.minimum(jnp.maximum(entries, -bound), bound).astype(held_as)


def setup_inputs(seed: int = 0) -> dict:
    splits = jax.random.split(jax.random.key(seed), 11)
    return {
        "voxel_feats": noise(splits[0], (BRICKS, 64, C), 1.0, 6.0, ((0, 32),)),
        "w_first": noise(splits[1], (27, C, C), (27 * C) ** -0.5, 0.109375),
        "w_second": noise(splits[2], (27, C, C), (27 * C) ** -0.5, 0.109375),
        "norm_gain": jnp.clip(1.0 + 0.1 * jax.random.normal(splits[3], (2, C), jnp.float32), 0.5, 1.5),
        "norm_shift": noise(splits[4], (2, C), 0.5, 3.0, (), jnp.float32),
        "grad_out": noise(splits[5], (BRICKS, 64, C), 1.0, 6.0, ((0, 32),)),
        "brick_count": draw_brick_count(jax.random.fold_in(splits[10], 71), 0),
        "kernel_map": draw_kernel_map(jax.random.fold_in(splits[10], 71), 0),
        "face_send": draw_face_send(jax.random.fold_in(splits[10], 71), 0),
        "corner_send": draw_corner_send(jax.random.fold_in(splits[10], 71), 0),
    }


TAP_LIST = [(a, b, c) for a in range(3) for b in range(3) for c in range(3)]
FACE_SIGNS = ((1, 0), (-1, 0), (0, 1), (0, -1))
CORNER_SIGNS = ((1, 1), (1, -1), (-1, 1), (-1, -1))
epsilon = 1e-05

def silu_slope(values):
    sigma = jax.nn.sigmoid(values)
    return sigma * (1.0 + values * (1.0 - sigma))

def source_range(e):
    if e < 0:
        return (slice(3, 4), slice(0, 1))
    if e == 0:
        return (slice(0, 4), slice(1, 5))
    return (slice(0, 1), slice(5, 6))

def assemble(extended, tile_table):
    planes = []
    for a in (-1, 0, 1):
        layers = []
        for b in (-1, 0, 1):
            pieces = []
            for c in (-1, 0, 1):
                d = 9 * (a + 1) + 3 * (b + 1) + (c + 1)
                region = extended[:, source_range(a)[0], source_range(b)[0], source_range(c)[0]]
                pieces.append(jnp.take(region, tile_table[:, d], axis=0))
            layers.append(jnp.concatenate(pieces, axis=3))
        planes.append(jnp.concatenate(layers, axis=2))
    return jnp.concatenate(planes, axis=1)

def patches(padded):
    bricks = padded.shape[0]
    channels = padded.shape[-1]
    return jnp.concatenate([padded[:, a:a + 4, b:b + 4, c:c + 4].reshape(bricks * 64, channels) for a, b, c in TAP_LIST], axis=1)

def spread(columns, bricks, channels):
    padded = jnp.zeros((bricks, 6, 6, 6, channels), jnp.float32)
    for k, (a, b, c) in enumerate(TAP_LIST):
        piece = columns[:, k * channels:(k + 1) * channels].reshape(bricks, 4, 4, 4, channels)
        padded = padded.at[:, a:a + 4, b:b + 4, c:c + 4].add(piece)
    return padded

def scatter_bricks(padded, tile_table, total):
    result = jnp.zeros((total, 4, 4, 4, padded.shape[-1]), jnp.float32)
    for a in (-1, 0, 1):
        for b in (-1, 0, 1):
            for c in (-1, 0, 1):
                d = 9 * (a + 1) + 3 * (b + 1) + (c + 1)
                range_a = source_range(a)
                range_b = source_range(b)
                range_c = source_range(c)
                result = result.at[tile_table[:, d], range_a[0], range_b[0], range_c[0]].add(padded[:, range_a[1], range_b[1], range_c[1]])
    return result

def moved(grid, shift_x, shift_y):
    widths = [(1, 1), (1, 1)] + [(0, 0)] * (grid.ndim - 2)
    padded = jnp.pad(grid, widths)
    return padded[1 - shift_x:1 - shift_x + N_GX, 1 - shift_y:1 - shift_y + N_GY]

def take_lists(field, lists):
    return jax.vmap(lambda tile_field, picks: jnp.take(tile_field, picks, axis=0))(field, lists)

def extend_all(field, face_send, corner_send):
    pieces = [field]
    for k in range(4):
        sent = take_lists(field, face_send[:, k])
        grid = sent.reshape((N_GX, N_GY) + sent.shape[1:])
        pieces.append(moved(grid, FACE_SIGNS[k][0], FACE_SIGNS[k][1]).reshape(sent.shape))
    for k in range(4):
        sent = take_lists(field, corner_send[:, k])
        grid = sent.reshape((N_GX, N_GY) + sent.shape[1:])
        pieces.append(moved(grid, CORNER_SIGNS[k][0], CORNER_SIGNS[k][1]).reshape(sent.shape))
    pieces.append(jnp.zeros((TILES, 1) + field.shape[2:], field.dtype))
    return jnp.concatenate(pieces, axis=1)

def add_lists(accum, lists, values):
    return jax.vmap(lambda tile_acc, picks, vals: tile_acc.at[picks].add(vals))(accum, lists, values)

def return_all(ext_grads, face_send, corner_send):
    result = ext_grads[:, :NB]
    for k in range(4):
        piece = ext_grads[:, NB + k * SF:NB + (k + 1) * SF]
        grid = piece.reshape((N_GX, N_GY) + piece.shape[1:])
        homed = moved(grid, -FACE_SIGNS[k][0], -FACE_SIGNS[k][1]).reshape(piece.shape)
        result = add_lists(result, face_send[:, k], homed)
    start = NB + 4 * SF
    for k in range(4):
        piece = ext_grads[:, start + k * SC:start + (k + 1) * SC]
        grid = piece.reshape((N_GX, N_GY) + piece.shape[1:])
        homed = moved(grid, -CORNER_SIGNS[k][0], -CORNER_SIGNS[k][1]).reshape(piece.shape)
        result = add_lists(result, corner_send[:, k], homed)
    return result

def forward_conv(extended, tables, weight):
    channels = weight.shape[2]
    flat = weight.reshape(27 * channels, channels)

    def single(pair):
        return jnp.dot(patches(assemble(pair[0], pair[1])), flat, preferred_element_type=jnp.float32)
    return lax.map(single, (extended, tables))

def backward_conv(extended, tables, grads, weight):
    channels = weight.shape[2]
    flat = weight.reshape(27 * channels, channels)

    def single(carry, items):
        columns = patches(assemble(items[0], items[1]))
        carry = carry + lax.dot_general(columns, items[2], (((0,), (0,)), ((), ())), preferred_element_type=jnp.float32)
        spread_cols = lax.dot_general(items[2], flat, (((1,), (1,)), ((), ())), preferred_element_type=jnp.float32)
        return (carry, scatter_bricks(spread(spread_cols, NB, channels), items[1], EXT))
    return lax.scan(single, jnp.zeros((27 * channels, channels), jnp.float32), (extended, tables, grads))

def normalize(values, occupied, voxels):
    center = lax.optimization_barrier(jnp.sum(values * occupied, axis=(0, 1))) / voxels
    spread_sq = lax.optimization_barrier(jnp.sum(values * values * occupied, axis=(0, 1))) / voxels - center * center
    recip = lax.rsqrt(spread_sq + epsilon)
    return ((values - center) * recip, recip)

def reference(voxel_feats, w_first, w_second, norm_gain, norm_shift, grad_out, brick_count, kernel_map, face_send, corner_send):
    channels = voxel_feats.shape[2]
    shape_five = (TILES, NB, 4, 4, 4, channels)
    tables = kernel_map.reshape(TILES, NB, 27)
    occupied = (jnp.arange(NB, dtype=jnp.int32)[None, :] < brick_count[:, None]).astype(jnp.float32)
    occupied = jnp.repeat(occupied, 64, axis=1)[:, :, None]
    feats = voxel_feats.reshape(TILES, NB * 64, channels) * occupied.astype(jnp.bfloat16)
    voxels = 64.0 * jnp.sum(brick_count.astype(jnp.float32))
    ext_one = extend_all(feats.reshape(shape_five), face_send, corner_send)
    z_one = forward_conv(ext_one, tables, w_first)
    xh_one, recip_one = normalize(z_one, occupied, voxels)
    u_one = norm_gain[0] * xh_one + norm_shift[0]
    a_one = (jax.nn.silu(u_one) * occupied).astype(jnp.bfloat16)
    ext_two = extend_all(a_one.reshape(shape_five), face_send, corner_send)
    z_two = forward_conv(ext_two, tables, w_second)
    xh_two, recip_two = normalize(z_two, occupied, voxels)
    pre = norm_gain[1] * xh_two + norm_shift[1] + feats.astype(jnp.float32)
    out_feats = (jax.nn.silu(pre) * occupied).astype(jnp.bfloat16)
    d_val = grad_out.reshape(TILES, NB * 64, channels).astype(jnp.float32) * occupied * silu_slope(pre)
    sum_two = lax.optimization_barrier(jnp.sum(d_val, axis=(0, 1)))
    cross_two = lax.optimization_barrier(jnp.sum(d_val * xh_two, axis=(0, 1)))
    dz_two = (occupied * norm_gain[1] * recip_two * (d_val - sum_two / voxels - xh_two * cross_two / voxels)).astype(jnp.bfloat16)
    dw_two, ge_two = backward_conv(ext_two, tables, dz_two, w_second)
    da_one = return_all(ge_two, face_send, corner_send).reshape(TILES, NB * 64, channels)
    du_one = da_one * occupied * silu_slope(u_one)
    sum_one = lax.optimization_barrier(jnp.sum(du_one, axis=(0, 1)))
    cross_one = lax.optimization_barrier(jnp.sum(du_one * xh_one, axis=(0, 1)))
    dz_one = (occupied * norm_gain[0] * recip_one * (du_one - sum_one / voxels - xh_one * cross_one / voxels)).astype(jnp.bfloat16)
    dw_one, ge_one = backward_conv(ext_one, tables, dz_one, w_first)
    back_in = return_all(ge_one, face_send, corner_send).reshape(TILES, NB * 64, channels)
    grad_in = ((d_val + back_in) * occupied).astype(jnp.bfloat16)
    root = jnp.sqrt(voxels)
    weight_grads = jnp.stack([dw_one, dw_two]).reshape(2, 27, channels, channels) / root
    norm_grads = jnp.stack([cross_one, sum_one, cross_two, sum_two]) / root
    return (out_feats.reshape(BRICKS, 64, channels), grad_in.reshape(BRICKS, 64, channels), weight_grads, norm_grads)
```

```python
import functools

import jax
import jax.numpy as jnp
import numpy as np
from jax import lax
from jax.experimental import pallas as pl
from jax.experimental.pallas import tpu as pltpu
from jax.sharding import PartitionSpec as P

MESH = pl.DeviceIdType.MESH
FACES = ((1, 0), (-1, 0), (0, 1), (0, -1))
CORNERS = ((1, 1), (1, -1), (-1, 1), (-1, -1))
epsilon = 1e-05
F32 = jnp.float32
BF16 = jnp.bfloat16


def plane_sources():
    direction = np.zeros((9, 16), np.int32)
    place = np.zeros((9, 16), np.int32)
    for s in range(9):
        for v in range(16):
            q, r = v // 4 + s // 3 - 1, v % 4 + s % 3 - 1
            oq, orr = (q >= 4) - (q < 0), (r >= 4) - (r < 0)
            direction[s, v] = 3 * (oq + 1) + orr + 1
            place[s, v] = 4 * (q - 4 * oq) + r - 4 * orr
    return direction.reshape(-1), place.reshape(-1)


def sigmoid(values):
    return 1.0 / (1.0 + jnp.exp(-values))


def slope(values):
    sigma = sigmoid(values)
    return sigma * (1.0 + values * (1.0 - sigma))


def dot(a, b, dims=((1,), (0,))):
    return lax.dot_general(a, b, (dims, ((), ())), preferred_element_type=F32)


def kernel(
    nx, ny, side, small,
    voxel_ref, w1_ref, w2_ref, gain_ref, shift_ref, grad_ref, count_ref, face_ref, corner_ref, rows_ref, cols_ref,
    out_ref, gin_ref, dw1_ref, dw2_ref, norms_ref,
    gather_ref, scatter_ref, mask_ref, fext_ref, zext_ref, zown_ref, eext_ref, q1_ref, q2_ref, d_ref,
    fsend_ref, zsend_ref, rsend_ref, ret_ref, xbuf_ref, ybuf_ref,
    halo_send, halo_recv, x_send, x_recv, y_send, y_recv,
):
    i, j = lax.axis_index("gx"), lax.axis_index("gy")
    bricks, _, _, channels = voxel_ref.shape
    entries = fext_ref.shape[0]
    vox = bricks * 64
    items = [(FACES[k], face_ref, k * side + t) for k in range(4) for t in range(side)]
    items += [(CORNERS[k], corner_ref, k * small + t) for k in range(4) for t in range(small)]

    def inside(dx, dy):
        ok = jnp.int32(1)
        if dx > 0:
            ok = ok * (i + 1 < nx).astype(jnp.int32)
        if dx < 0:
            ok = ok * (i > 0).astype(jnp.int32)
        if dy > 0:
            ok = ok * (j + 1 < ny).astype(jnp.int32)
        if dy < 0:
            ok = ok * (j > 0).astype(jnp.int32)
        return ok

    barrier = pltpu.get_barrier_semaphore()
    waits = jnp.int32(nx - 1 + ny - 1)
    for k in range(1, nx):
        pl.semaphore_signal(barrier, inc=1, device_id=(lax.rem(i + k, nx), j), device_id_type=MESH)
    for k in range(1, ny):
        pl.semaphore_signal(barrier, inc=1, device_id=(i, lax.rem(j + k, ny)), device_id_type=MESH)
    for dx, dy in CORNERS:
        there = inside(dx, dy)
        waits = waits + there

        @pl.when(there == 1)
        def _():
            pl.semaphore_signal(barrier, inc=1, device_id=(i + dx, j + dy), device_id_type=MESH)

    def halo(round_, n, src, dst, direction):
        dx, dy = direction
        return pltpu.make_async_remote_copy(
            src_ref=src, dst_ref=dst, send_sem=halo_send.at[round_, n], recv_sem=halo_recv.at[round_, n],
            device_id=(i + dx, j + dy), device_id_type=MESH,
        )

    def start_halo(round_, sources, targets, sign):
        for n, ((dx, dy), _, _) in enumerate(items):
            way = (sign * dx, sign * dy)

            @pl.when(inside(*way) == 1)
            def _():
                halo(round_, n, sources(n), targets(n), way).start()

    def end_halo(round_, sources, targets, sign):
        for n, ((dx, dy), _, _) in enumerate(items):
            way = (sign * dx, sign * dy)

            @pl.when(inside(-way[0], -way[1]) == 1)
            def _():
                halo(round_, n, sources(n), targets(n), (-way[0], -way[1])).wait_recv()

    def drain_halo(round_, sources, targets, sign):
        for n, ((dx, dy), _, _) in enumerate(items):
            way = (sign * dx, sign * dy)

            @pl.when(inside(*way) == 1)
            def _():
                halo(round_, n, sources(n), targets(n), way).wait_send()

    def x_copy(r, slot, k, to):
        return pltpu.make_async_remote_copy(
            src_ref=xbuf_ref.at[r, slot], dst_ref=xbuf_ref.at[r, slot], send_sem=x_send.at[r, k],
            recv_sem=x_recv.at[r, k], device_id=(to, j), device_id_type=MESH,
        )

    def y_copy(r, slot, k, to):
        return pltpu.make_async_remote_copy(
            src_ref=ybuf_ref.at[r, slot], dst_ref=ybuf_ref.at[r, slot], send_sem=y_send.at[r, k],
            recv_sem=y_recv.at[r, k], device_id=(i, to), device_id_type=MESH,
        )

    def start_sums(r, rows):
        slab = jnp.concatenate(rows + [jnp.zeros((8 - len(rows), channels), F32)], axis=0)
        xbuf_ref[r, i] = slab
        for k in range(1, nx):
            x_copy(r, i, k, lax.rem(i + k, nx)).start()

    def end_sums(r):
        for k in range(1, nx):
            x_copy(r, lax.rem(i - k + nx, nx), k, i).wait_recv()
        ybuf_ref[r, j] = jnp.sum(xbuf_ref[r], axis=0)
        for k in range(1, ny):
            y_copy(r, j, k, lax.rem(j + k, ny)).start()
        for k in range(1, ny):
            y_copy(r, lax.rem(j - k + ny, ny), k, j).wait_recv()
        return jnp.sum(ybuf_ref[r], axis=0)

    def drain_sums(r):
        for k in range(1, nx):
            x_copy(r, i, k, lax.rem(i + k, nx)).wait_send()
        for k in range(1, ny):
            y_copy(r, j, k, lax.rem(j + k, ny)).wait_send()

    def colsum(values):
        return jnp.sum(values, axis=0, keepdims=True)

    count = count_ref[0]
    entry = lax.broadcasted_iota(jnp.int32, mask_ref.shape, 0)
    mask = jnp.where(entry < count, 1.0, 0.0)
    mask = jnp.where(entry < bricks, mask, 0.0)
    for n, ((dx, dy), _, _) in enumerate(items):
        mask = jnp.where(entry == bricks + n, inside(-dx, -dy).astype(F32), mask)
    mask_ref[...] = mask
    fext_ref[:bricks] = (voxel_ref[...].astype(F32) * mask_ref[:bricks]).astype(BF16)
    for n, (_, list_ref, place) in enumerate(items):
        fsend_ref[n] = voxel_ref[list_ref[place]]
    pl.semaphore_wait(barrier, waits)
    features = (0, lambda n: fsend_ref.at[n], lambda n: fext_ref.at[bricks + n], 1)
    start_halo(*features)

    for o in range(3):
        lane = lax.broadcasted_iota(jnp.int32, gather_ref.shape[1:], 1)
        gather_ref[o] = jnp.where(lane == rows_ref[:, o : o + 1], 1.0, 0.0).astype(BF16)
        row = lax.broadcasted_iota(jnp.int32, scatter_ref.shape[1:], 0)
        scatter_ref[o] = jnp.where(row == cols_ref[o : o + 1, :], 1.0, 0.0).astype(BF16)

    def collect(field, q_ref):
        flat = [field[:, p].reshape(entries * 16, channels) for p in range(4)]
        low = dot(gather_ref[0], flat[3]).astype(BF16)
        mid = dot(gather_ref[1], jnp.concatenate(flat, axis=1)).astype(BF16)
        high = dot(gather_ref[2], flat[0]).astype(BF16)
        planes = [low] + [mid[:, p * channels : (p + 1) * channels] for p in range(4)] + [high]
        for a, plane in enumerate(planes):
            plane = plane.reshape(bricks, 9, 16, channels)
            for s in range(9):
                q_ref[:, a, :, s * channels : (s + 1) * channels] = plane[:, s]

    width = 9 * channels

    def taps(q_ref, a):
        return q_ref[:, a : a + 4].reshape(vox, width)

    def conv(q_ref, w_ref):
        total = dot(taps(q_ref, 0), w_ref[:width])
        for a in (1, 2):
            total = total + dot(taps(q_ref, a), w_ref[a * width : (a + 1) * width])
        return total

    def conv_weights(q_ref, grads, scale, dw_ref):
        for a in range(3):
            dw_ref[a * width : (a + 1) * width] = dot(taps(q_ref, a), grads, ((0,), (0,))) * scale

    def conv_back(grads, w_ref):
        parts = [
            dot(grads, w_ref[a * width : (a + 1) * width], ((1,), (1,))).reshape(bricks, 4, 16, width)
            for a in range(3)
        ]
        for a6 in range(6):
            piece = None
            for a in range(3):
                if 0 <= a6 - a < 4:
                    term = parts[a][:, a6 - a]
                    piece = term if piece is None else piece + term
            for s in range(9):
                d_ref[a6, :, s] = piece[:, :, s * channels : (s + 1) * channels]

        def spread(o, planes):
            value = [d_ref[a6].reshape(bricks * 144, channels) for a6 in planes]
            value = value[0] if len(value) == 1 else jnp.concatenate(value, axis=1)
            upper = value.astype(BF16)
            lower = (value - upper.astype(F32)).astype(BF16)
            return dot(scatter_ref[o], upper) + dot(scatter_ref[o], lower)

        mid = spread(1, (1, 2, 3, 4))
        low, high = spread(0, (0,)), spread(2, (5,))
        for p in range(4):
            value = mid[:, p * channels : (p + 1) * channels]
            if p == 3:
                value = value + low
            if p == 0:
                value = value + high
            eext_ref[:, p] = value.reshape(entries, 16, channels)

    def home(values):
        brick = lax.broadcasted_iota(jnp.int32, values.shape, 0)
        for n, ((dx, dy), list_ref, place) in enumerate(items):
            chosen = jnp.where(inside(dx, dy) == 1, list_ref[place], -1)
            values = values + jnp.where(brick == chosen, ret_ref[ret_base[0] + n].astype(F32)[None], 0.0)
        return values

    ret_base = [0]
    sent = len(items)

    end_halo(*features)
    fext_ref[bricks:] = jnp.where(mask_ref[bricks:] > 0.0, fext_ref[bricks:].astype(F32), 0.0).astype(BF16)
    collect(fext_ref, q1_ref)
    z1 = conv(q1_ref, w1_ref)
    zown_ref[...] = z1.reshape(bricks, 4, 16, channels)
    for n, (_, list_ref, place) in enumerate(items):
        zsend_ref[n] = zown_ref[list_ref[place]]
    raw = (1, lambda n: zsend_ref.at[n], lambda n: zext_ref.at[bricks + n], 1)
    occupied = mask_ref[:bricks].reshape(vox, channels)
    weighted = jnp.zeros((1, channels), F32) + 64.0 * count.astype(F32)
    start_sums(0, [colsum(z1 * occupied), colsum(z1 * z1 * occupied), weighted])
    start_halo(*raw)
    totals = end_sums(0)
    voxels = totals[2:3]
    mean1 = totals[0:1] / voxels
    recip1 = lax.rsqrt(totals[1:2] / voxels - mean1 * mean1 + epsilon)
    end_halo(*raw)

    gain1, gain2 = gain_ref[0:1], gain_ref[1:2]
    shift1, shift2 = shift_ref[0:1], shift_ref[1:2]
    wide = mask_ref[...].reshape(entries * 64, channels)
    zext_ref[:bricks] = zown_ref[...]
    zall = jnp.where(wide > 0.0, zext_ref[...].reshape(entries * 64, channels), 0.0)
    xh1 = (zall - mean1) * recip1
    zext_ref[...] = xh1.reshape(zext_ref.shape)
    u1 = gain1 * xh1 + shift1
    a1 = (u1 * sigmoid(u1) * wide).astype(BF16)
    collect(a1.reshape(entries, 4, 16, channels), q2_ref)
    z2 = conv(q2_ref, w2_ref)
    start_sums(1, [colsum(z2 * occupied), colsum(z2 * z2 * occupied)])
    totals = end_sums(1)
    mean2 = totals[0:1] / voxels
    recip2 = lax.rsqrt(totals[1:2] / voxels - mean2 * mean2 + epsilon)
    xh2 = (z2 - mean2) * recip2
    feats = fext_ref[:bricks].astype(F32).reshape(vox, channels)
    pre = gain2 * xh2 + shift2 + feats
    dv = grad_ref[...].astype(F32).reshape(vox, channels) * occupied * slope(pre)
    start_sums(2, [colsum(dv), colsum(dv * xh2)])
    out_ref[...] = (pre * sigmoid(pre) * occupied).astype(BF16).reshape(out_ref.shape)
    totals = end_sums(2)
    sd2, sx2 = totals[0:1], totals[1:2]
    dz2 = (occupied * gain2 * recip2 * (dv - sd2 / voxels - xh2 * (sx2 / voxels))).astype(BF16)
    root = lax.rsqrt(voxels)

    conv_back(dz2, w2_ref)
    rsend_ref[:sent] = eext_ref[bricks:].astype(BF16)
    back2 = (2, lambda n: rsend_ref.at[n], lambda n: ret_ref.at[n], -1)
    start_halo(*back2)
    xh1 = zext_ref[...].reshape(entries * 64, channels)
    part = eext_ref[...].reshape(entries * 64, channels) * wide * slope(gain1 * xh1 + shift1)
    start_sums(3, [colsum(part), colsum(part * xh1)])
    conv_weights(q2_ref, dz2, root, dw2_ref)
    totals = end_sums(3)
    sd1, sx1 = totals[0:1], totals[1:2]
    norms_ref[...] = jnp.concatenate([sx1, sd1, sx2, sd2], axis=0) * root
    end_halo(*back2)
    da1 = home(eext_ref[:bricks]).reshape(vox, channels)
    xh1 = zext_ref[:bricks].reshape(vox, channels)
    du1 = da1 * occupied * slope(gain1 * xh1 + shift1)
    dz1 = (occupied * gain1 * recip1 * (du1 - sd1 / voxels - xh1 * (sx1 / voxels))).astype(BF16)

    conv_back(dz1, w1_ref)
    rsend_ref[sent:] = eext_ref[bricks:].astype(BF16)
    back1 = (3, lambda n: rsend_ref.at[sent + n], lambda n: ret_ref.at[sent + n], -1)
    start_halo(*back1)
    conv_weights(q1_ref, dz1, root, dw1_ref)
    end_halo(*back1)
    ret_base[0] = sent
    back_in = home(eext_ref[:bricks]).reshape(vox, channels)
    gin_ref[...] = ((dv + back_in) * occupied).astype(BF16).reshape(gin_ref.shape)
    for way in (features, raw, back2, back1):
        drain_halo(*way)
    for r in range(4):
        drain_sums(r)


def solution(mesh):
    nx, ny = mesh.shape["gx"], mesh.shape["gy"]
    direction, place = plane_sources()

    def body(voxel, w1, w2, gain, shift, grad_out, brick_count, kernel_map, face_send, corner_send):
        bricks, _, channels = voxel.shape
        side, small = face_send.shape[2], corner_send.shape[2]
        sent = 4 * side + 4 * small
        entries = bricks + sent
        field = (bricks, 4, 16, channels)
        rows = bricks * 144
        targets = jnp.stack(
            [(kernel_map[:, 9 * o + direction] * 16 + place).reshape(rows) for o in range(3)], axis=0
        )
        vmem, smem = pl.BlockSpec(memory_space=pltpu.VMEM), pl.BlockSpec(memory_space=pltpu.SMEM)
        taps = w1.shape[0] * channels
        out, gin, dw1, dw2, norms = pl.pallas_call(
            functools.partial(kernel, nx, ny, side, small),
            out_shape=[
                jax.ShapeDtypeStruct(field, BF16),
                jax.ShapeDtypeStruct(field, BF16),
                jax.ShapeDtypeStruct((taps, channels), F32),
                jax.ShapeDtypeStruct((taps, channels), F32),
                jax.ShapeDtypeStruct((4, channels), F32),
            ],
            in_specs=[vmem] * 6 + [smem] * 3 + [vmem] * 2,
            out_specs=[vmem] * 5,
            scratch_shapes=[
                pltpu.VMEM((3, rows, entries * 16), BF16),
                pltpu.VMEM((3, entries * 16, rows), BF16),
                pltpu.VMEM((entries, 4, 16, channels), F32),
                pltpu.VMEM((entries, 4, 16, channels), BF16),
                pltpu.VMEM((entries, 4, 16, channels), F32),
                pltpu.VMEM((bricks, 4, 16, channels), F32),
                pltpu.VMEM((entries, 4, 16, channels), F32),
                pltpu.VMEM((bricks, 6, 16, 9 * channels), BF16),
                pltpu.VMEM((bricks, 6, 16, 9 * channels), BF16),
                pltpu.VMEM((6, bricks, 9, 16, channels), F32),
                pltpu.VMEM((sent, 4, 16, channels), BF16),
                pltpu.VMEM((sent, 4, 16, channels), F32),
                pltpu.VMEM((2 * sent, 4, 16, channels), BF16),
                pltpu.VMEM((2 * sent, 4, 16, channels), BF16),
                pltpu.VMEM((4, nx, 8, channels), F32),
                pltpu.VMEM((4, ny, 8, channels), F32),
                pltpu.SemaphoreType.DMA((4, sent)),
                pltpu.SemaphoreType.DMA((4, sent)),
                pltpu.SemaphoreType.DMA((4, nx)),
                pltpu.SemaphoreType.DMA((4, nx)),
                pltpu.SemaphoreType.DMA((4, ny)),
                pltpu.SemaphoreType.DMA((4, ny)),
            ],
            compiler_params=pltpu.CompilerParams(
                collective_id=0, has_side_effects=True, vmem_limit_bytes=50 * 1024 * 1024
            ),
        )(
            voxel.reshape(field), w1.reshape(taps, channels), w2.reshape(taps, channels), gain, shift,
            grad_out.reshape(field), brick_count, face_send.reshape(-1), corner_send.reshape(-1),
            targets.T, targets,
        )
        dw1, dw2 = lax.psum((dw1, dw2), ("gx", "gy"))
        weight_grads = jnp.stack([dw1, dw2]).reshape((2,) + w1.shape)
        return out.reshape(voxel.shape), gin.reshape(voxel.shape), weight_grads, norms

    tiles = P(("gx", "gy"))
    in_specs = (tiles, P(), P(), P(), P(), tiles, tiles, tiles, tiles, tiles)
    return jax.shard_map(
        body, mesh=mesh, in_specs=in_specs, out_specs=(tiles, tiles, P(), P()), check_vma=False
    )
```

```python
import functools

import jax
import jax.numpy as jnp
from jax import lax
from jax.experimental import pallas as pl
from jax.experimental.pallas import tpu as pltpu
from jax.sharding import PartitionSpec as P

MESH = pl.DeviceIdType.MESH
FACES = ((1, 0), (-1, 0), (0, 1), (0, -1))
CORNERS = ((1, 1), (1, -1), (-1, 1), (-1, -1))
epsilon = 1e-05
F32 = jnp.float32
BF16 = jnp.bfloat16


def plane_sources(at):
    s, q, r = at >> 4, (at >> 2) & 3, at & 3
    tens = jnp.where(s >= 6, 2, jnp.where(s >= 3, 1, 0))
    q, r = q + tens - 1, r + s - 3 * tens - 1
    oq = jnp.where(q > 3, 1, jnp.where(q < 0, -1, 0))
    orr = jnp.where(r > 3, 1, jnp.where(r < 0, -1, 0))
    return 3 * (oq + 1) + orr + 1, 4 * (q - 4 * oq) + r - 4 * orr


def sigmoid(values):
    return 1.0 / (1.0 + jnp.exp(-values))


def slope(values):
    sigma = sigmoid(values)
    return sigma * (1.0 + values * (1.0 - sigma))


def dot(a, b, dims=((1,), (0,))):
    return lax.dot_general(a, b, (dims, ((), ())), preferred_element_type=F32)


def kernel(
    nx, ny, side, small,
    voxel_ref, w1_hbm, w2_hbm, gain_ref, shift_ref, grad_hbm, count_ref, map_ref, face_ref, corner_ref,
    out_ref, gin_ref, dw_ref, norms_ref,
    w1_ref, w2_ref, grad_ref, load_sem,
    gather_ref, scatter_ref, mask_ref, fext_ref, zext_ref, zown_ref, eext_ref, q1_ref, q2_ref, d_ref,
    fsend_ref, zsend_ref, rsend_ref, ret_ref, xbuf_ref, ybuf_ref,
    halo_send, halo_recv, x_send, x_recv, y_send, y_recv,
    part_ref, pair_ref, half_ref, cross_ref, quarter_ref, deep_ref, full_ref,
    pair_send, pair_recv, cross_send, cross_recv, deep_send, deep_recv,
):
    i, j = lax.axis_index("gx"), lax.axis_index("gy")
    bricks, _, _, channels = voxel_ref.shape
    entries = fext_ref.shape[0]
    vox = bricks * 64
    items = [(FACES[k], face_ref, k, t) for k in range(4) for t in range(side)]
    items += [(CORNERS[k], corner_ref, k, t) for k in range(4) for t in range(small)]

    def inside(dx, dy):
        ok = jnp.int32(1)
        if dx > 0:
            ok = ok * (i + 1 < nx).astype(jnp.int32)
        if dx < 0:
            ok = ok * (i > 0).astype(jnp.int32)
        if dy > 0:
            ok = ok * (j + 1 < ny).astype(jnp.int32)
        if dy < 0:
            ok = ok * (j > 0).astype(jnp.int32)
        return ok

    barrier = pltpu.get_barrier_semaphore()
    loads = [
        pltpu.make_async_copy(source, target, load_sem.at[n])
        for n, (source, target) in enumerate([(w1_hbm, w1_ref), (w2_hbm, w2_ref), (grad_hbm, grad_ref)])
    ]
    for load in loads:
        load.start()
    waits = jnp.int32(nx - 1 + ny - 1)
    for k in range(1, nx):
        pl.semaphore_signal(barrier, inc=1, device_id=(lax.rem(i + k, nx), j), device_id_type=MESH)
    for k in range(1, ny):
        pl.semaphore_signal(barrier, inc=1, device_id=(i, lax.rem(j + k, ny)), device_id_type=MESH)
    for dx, dy in CORNERS:
        there = inside(dx, dy)
        waits = waits + there

        @pl.when(there == 1)
        def _():
            pl.semaphore_signal(barrier, inc=1, device_id=(i + dx, j + dy), device_id_type=MESH)

    def halo(round_, n, src, dst, direction):
        dx, dy = direction
        return pltpu.make_async_remote_copy(
            src_ref=src, dst_ref=dst, send_sem=halo_send.at[round_, n], recv_sem=halo_recv.at[round_, n],
            device_id=(i + dx, j + dy), device_id_type=MESH,
        )

    def start_halo(round_, sources, targets, sign):
        for n, ((dx, dy), _, _, _) in enumerate(items):
            way = (sign * dx, sign * dy)

            @pl.when(inside(*way) == 1)
            def _():
                halo(round_, n, sources(n), targets(n), way).start()

    def end_halo(round_, sources, targets, sign):
        for n, ((dx, dy), _, _, _) in enumerate(items):
            way = (sign * dx, sign * dy)

            @pl.when(inside(-way[0], -way[1]) == 1)
            def _():
                halo(round_, n, sources(n), targets(n), (-way[0], -way[1])).wait_recv()

    def drain_halo(round_, sources, targets, sign):
        for n, ((dx, dy), _, _, _) in enumerate(items):
            way = (sign * dx, sign * dy)

            @pl.when(inside(*way) == 1)
            def _():
                halo(round_, n, sources(n), targets(n), way).wait_send()

    def x_copy(r, slot, k, to):
        return pltpu.make_async_remote_copy(
            src_ref=xbuf_ref.at[r, slot], dst_ref=xbuf_ref.at[r, slot], send_sem=x_send.at[r, k],
            recv_sem=x_recv.at[r, k], device_id=(to, j), device_id_type=MESH,
        )

    def y_copy(r, slot, k, to):
        return pltpu.make_async_remote_copy(
            src_ref=ybuf_ref.at[r, slot], dst_ref=ybuf_ref.at[r, slot], send_sem=y_send.at[r, k],
            recv_sem=y_recv.at[r, k], device_id=(i, to), device_id_type=MESH,
        )

    def start_sums(r, rows):
        slab = jnp.concatenate(rows + [jnp.zeros((8 - len(rows), channels), F32)], axis=0)
        xbuf_ref[r, i] = slab
        for k in range(1, nx):
            x_copy(r, i, k, lax.rem(i + k, nx)).start()

    def end_sums(r):
        for k in range(1, nx):
            x_copy(r, lax.rem(i - k + nx, nx), k, i).wait_recv()
        ybuf_ref[r, j] = jnp.sum(xbuf_ref[r], axis=0)
        for k in range(1, ny):
            y_copy(r, j, k, lax.rem(j + k, ny)).start()
        for k in range(1, ny):
            y_copy(r, lax.rem(j - k + ny, ny), k, j).wait_recv()
        return jnp.sum(ybuf_ref[r], axis=0)

    def drain_sums(r):
        for k in range(1, nx):
            x_copy(r, i, k, lax.rem(i + k, nx)).wait_send()
        for k in range(1, ny):
            y_copy(r, j, k, lax.rem(j + k, ny)).wait_send()

    def colsum(values):
        return jnp.sum(values, axis=0, keepdims=True)

    count = count_ref[0]
    entry = lax.broadcasted_iota(jnp.int32, mask_ref.shape, 0)
    mask = jnp.where(entry < count, 1.0, 0.0)
    mask = jnp.where(entry < bricks, mask, 0.0)
    for n, ((dx, dy), _, _, _) in enumerate(items):
        mask = jnp.where(entry == bricks + n, inside(-dx, -dy).astype(F32), mask)
    mask_ref[...] = mask
    fext_ref[:bricks] = (voxel_ref[...].astype(F32) * mask_ref[:bricks]).astype(BF16)
    for n, (_, list_ref, k, t) in enumerate(items):
        fsend_ref[n] = voxel_ref[list_ref[0, k, t]]
    pl.semaphore_wait(barrier, waits)
    features = (0, lambda n: fsend_ref.at[n], lambda n: fext_ref.at[bricks + n], 1)
    start_halo(*features)

    lane = lax.broadcasted_iota(jnp.int32, (144, entries * 16), 1)
    row = lax.broadcasted_iota(jnp.int32, scatter_ref.shape[1:], 0)
    down, down_place = plane_sources(lax.broadcasted_iota(jnp.int32, (144, 1), 0))
    across = lax.broadcasted_iota(jnp.int32, (1, bricks * 144), 1)
    owner = jnp.zeros_like(across)
    for b in range(1, bricks):
        owner = owner + jnp.where(across >= b * 144, 1, 0)
    along, along_place = plane_sources(across - 144 * owner)
    along = along + 9 * owner
    for o in range(3):
        tall = along_place
        for b in range(bricks):
            target = down_place
            for d in range(9):
                start = 16 * map_ref[b, 9 * o + d]
                target = target + jnp.where(down == d, start, 0)
                tall = tall + jnp.where(along == 9 * b + d, start, 0)
            gather_ref[o, b * 144 : (b + 1) * 144] = jnp.where(lane == target, 1.0, 0.0).astype(BF16)
        scatter_ref[o] = jnp.where(row == tall, 1.0, 0.0).astype(BF16)

    def collect(field, q_ref):
        flat = [field[:, p].reshape(entries * 16, channels) for p in range(4)]
        low = dot(gather_ref[0], flat[3]).astype(BF16)
        mid = dot(gather_ref[1], jnp.concatenate(flat, axis=1)).astype(BF16)
        high = dot(gather_ref[2], flat[0]).astype(BF16)
        planes = [low] + [mid[:, p * channels : (p + 1) * channels] for p in range(4)] + [high]
        for a, plane in enumerate(planes):
            plane = plane.reshape(bricks, 9, 16, channels)
            for s in range(9):
                q_ref[:, a, :, s * channels : (s + 1) * channels] = plane[:, s]

    width = 9 * channels

    def taps(q_ref, a):
        return q_ref[:, a : a + 4].reshape(vox, width)

    def conv(q_ref, w_ref):
        total = dot(taps(q_ref, 0), w_ref[:width])
        for a in (1, 2):
            total = total + dot(taps(q_ref, a), w_ref[a * width : (a + 1) * width])
        return total

    def conv_weights(w, q_ref, grads, scale):
        for a in range(3):
            value = dot(taps(q_ref, a), grads, ((0,), (0,))) * scale
            part_ref[w, a * width : (a + 1) * width] = value.astype(BF16)
        if part_ref.shape[1] > 3 * width:
            part_ref[w, 3 * width :] = jnp.zeros((part_ref.shape[1] - 3 * width, channels), BF16)

    nz = ny // 2
    mate = lax.rem(j, 2)
    level = j // 2
    chunk = deep_ref.shape[2]
    half = part_ref.shape[1] // 2

    def pair_copy(w, way):
        if way == 0:
            source = part_ref.at[w, pl.ds(pl.multiple_of((1 - mate) * half, 16), half)]
            target = pair_ref.at[w]
        else:
            source = target = full_ref.at[w, mate]
        return pltpu.make_async_remote_copy(
            src_ref=source, dst_ref=target, send_sem=pair_send.at[w, way], recv_sem=pair_recv.at[w, way],
            device_id=(i, j + 1 - 2 * mate), device_id_type=MESH,
        )

    def pair_wait(w, way):
        target = pair_ref.at[w] if way == 0 else full_ref.at[w, 1 - mate]
        pltpu.make_async_remote_copy(
            src_ref=target, dst_ref=target, send_sem=pair_send.at[w, way], recv_sem=pair_recv.at[w, way],
            device_id=(i, j + 1 - 2 * mate), device_id_type=MESH,
        ).wait_recv()

    def cross_copy(w, way, k, receive):
        to = lax.rem(i + k, nx)
        slot = lax.rem(i - k + nx, nx) if receive else i
        target = full_ref.at[w, mate, slot] if way else cross_ref.at[w, slot]
        source = target if way or receive else half_ref.at[w, to]
        return pltpu.make_async_remote_copy(
            src_ref=source, dst_ref=target, send_sem=cross_send.at[w, way, k], recv_sem=cross_recv.at[w, way, k],
            device_id=(to, j), device_id_type=MESH,
        )

    def deep_copy(w, way, k, receive):
        to = lax.rem(level + k, nz)
        slot = lax.rem(level - k + nz, nz) if receive else level
        target = full_ref.at[w, mate, i, slot] if way else deep_ref.at[w, slot]
        source = target if way or receive else quarter_ref.at[w, to]
        return pltpu.make_async_remote_copy(
            src_ref=source, dst_ref=target, send_sem=deep_send.at[w, way, k], recv_sem=deep_recv.at[w, way, k],
            device_id=(i, 2 * to + mate), device_id_type=MESH,
        )

    def reduce_step(w, step):
        if step == 0:
            pair_copy(w, 0).start()
        if step == 1:
            pair_wait(w, 0)
            own = part_ref[w, pl.ds(pl.multiple_of(mate * half, 16), half)]
            value = own.astype(F32) + pair_ref[w].astype(F32)
            half_ref[w] = value.astype(BF16).reshape(half_ref.shape[1:])
            for k in range(1, nx):
                cross_copy(w, 0, k, False).start()
            cross_ref[w, i] = half_ref[w, i]
        if step == 2:
            for k in range(1, nx):
                cross_copy(w, 0, k, True).wait_recv()
            value = jnp.sum(cross_ref[w].astype(F32), axis=0)
            quarter_ref[w] = value.astype(BF16).reshape(quarter_ref.shape[1:])
            for k in range(1, nz):
                deep_copy(w, 0, k, False).start()
            deep_ref[w, level] = quarter_ref[w, level]
        if step == 3:
            for k in range(1, nz):
                deep_copy(w, 0, k, True).wait_recv()
            full_ref[w, mate, i, level] = jnp.sum(deep_ref[w].astype(F32), axis=0).astype(BF16)
            for k in range(1, nz):
                deep_copy(w, 1, k, False).start()
        if step == 4:
            for k in range(1, nz):
                deep_copy(w, 1, k, True).wait_recv()
            for k in range(1, nx):
                cross_copy(w, 1, k, False).start()
        if step == 5:
            for k in range(1, nx):
                cross_copy(w, 1, k, True).wait_recv()
            pair_copy(w, 1).start()
        if step == 6:
            pair_wait(w, 1)
            dw_ref[w] = full_ref[w].reshape(dw_ref.shape[1:])

    def drain_reduce(w):
        for way in range(2):
            pair_copy(w, way).wait_send()
            for k in range(1, nx):
                cross_copy(w, way, k, False).wait_send()
            for k in range(1, nz):
                deep_copy(w, way, k, False).wait_send()

    def conv_back(grads, w_ref):
        parts = [
            dot(grads, w_ref[a * width : (a + 1) * width], ((1,), (1,))).reshape(bricks, 4, 16, width)
            for a in range(3)
        ]
        for a6 in range(6):
            piece = None
            for a in range(3):
                if 0 <= a6 - a < 4:
                    term = parts[a][:, a6 - a]
                    piece = term if piece is None else piece + term
            for s in range(9):
                d_ref[a6, :, s] = piece[:, :, s * channels : (s + 1) * channels]

        def spread(o, planes):
            value = [d_ref[a6].reshape(bricks * 144, channels) for a6 in planes]
            value = value[0] if len(value) == 1 else jnp.concatenate(value, axis=1)
            upper = value.astype(BF16)
            lower = (value - upper.astype(F32)).astype(BF16)
            return dot(scatter_ref[o], upper) + dot(scatter_ref[o], lower)

        mid = spread(1, (1, 2, 3, 4))
        low, high = spread(0, (0,)), spread(2, (5,))
        for p in range(4):
            value = mid[:, p * channels : (p + 1) * channels]
            if p == 3:
                value = value + low
            if p == 0:
                value = value + high
            eext_ref[:, p] = value.reshape(entries, 16, channels)

    def home(values):
        brick = lax.broadcasted_iota(jnp.int32, values.shape, 0)
        for n, ((dx, dy), list_ref, k, t) in enumerate(items):
            chosen = jnp.where(inside(dx, dy) == 1, list_ref[0, k, t], -1)
            values = values + jnp.where(brick == chosen, ret_ref[ret_base[0] + n].astype(F32)[None], 0.0)
        return values

    ret_base = [0]
    sent = len(items)

    end_halo(*features)
    fext_ref[bricks:] = jnp.where(mask_ref[bricks:] > 0.0, fext_ref[bricks:].astype(F32), 0.0).astype(BF16)
    collect(fext_ref, q1_ref)
    loads[0].wait()
    z1 = conv(q1_ref, w1_ref)
    zown_ref[...] = z1.reshape(bricks, 4, 16, channels)
    for n, (_, list_ref, k, t) in enumerate(items):
        zsend_ref[n] = zown_ref[list_ref[0, k, t]]
    raw = (1, lambda n: zsend_ref.at[n], lambda n: zext_ref.at[bricks + n], 1)
    occupied = mask_ref[:bricks].reshape(vox, channels)
    weighted = jnp.zeros((1, channels), F32) + 64.0 * count.astype(F32)
    start_sums(0, [colsum(z1 * occupied), colsum(z1 * z1 * occupied), weighted])
    start_halo(*raw)
    totals = end_sums(0)
    voxels = totals[2:3]
    mean1 = totals[0:1] / voxels
    recip1 = lax.rsqrt(totals[1:2] / voxels - mean1 * mean1 + epsilon)
    end_halo(*raw)

    gain1, gain2 = gain_ref[0:1], gain_ref[1:2]
    shift1, shift2 = shift_ref[0:1], shift_ref[1:2]
    wide = mask_ref[...].reshape(entries * 64, channels)
    zext_ref[:bricks] = zown_ref[...]
    zall = jnp.where(wide > 0.0, zext_ref[...].reshape(entries * 64, channels), 0.0)
    xh1 = (zall - mean1) * recip1
    zext_ref[...] = xh1.reshape(zext_ref.shape)
    u1 = gain1 * xh1 + shift1
    a1 = (u1 * sigmoid(u1) * wide).astype(BF16)
    collect(a1.reshape(entries, 4, 16, channels), q2_ref)
    loads[1].wait()
    z2 = conv(q2_ref, w2_ref)
    start_sums(1, [colsum(z2 * occupied), colsum(z2 * z2 * occupied)])
    totals = end_sums(1)
    mean2 = totals[0:1] / voxels
    recip2 = lax.rsqrt(totals[1:2] / voxels - mean2 * mean2 + epsilon)
    xh2 = (z2 - mean2) * recip2
    feats = fext_ref[:bricks].astype(F32).reshape(vox, channels)
    pre = gain2 * xh2 + shift2 + feats
    loads[2].wait()
    dv = grad_ref[...].astype(F32).reshape(vox, channels) * occupied * slope(pre)
    start_sums(2, [colsum(dv), colsum(dv * xh2)])
    out_ref[...] = (pre * sigmoid(pre) * occupied).astype(BF16).reshape(out_ref.shape)
    totals = end_sums(2)
    sd2, sx2 = totals[0:1], totals[1:2]
    dz2 = (occupied * gain2 * recip2 * (dv - sd2 / voxels - xh2 * (sx2 / voxels))).astype(BF16)
    root = lax.rsqrt(voxels)

    conv_back(dz2, w2_ref)
    rsend_ref[:sent] = eext_ref[bricks:].astype(BF16)
    back2 = (2, lambda n: rsend_ref.at[n], lambda n: ret_ref.at[n], -1)
    start_halo(*back2)
    xh1 = zext_ref[...].reshape(entries * 64, channels)
    part = eext_ref[...].reshape(entries * 64, channels) * wide * slope(gain1 * xh1 + shift1)
    start_sums(3, [colsum(part), colsum(part * xh1)])
    conv_weights(1, q2_ref, dz2, root)
    reduce_step(1, 0)
    totals = end_sums(3)
    reduce_step(1, 1)
    sd1, sx1 = totals[0:1], totals[1:2]
    norms_ref[...] = jnp.concatenate([sx1, sd1, sx2, sd2], axis=0) * root
    end_halo(*back2)
    da1 = home(eext_ref[:bricks]).reshape(vox, channels)
    xh1 = zext_ref[:bricks].reshape(vox, channels)
    du1 = da1 * occupied * slope(gain1 * xh1 + shift1)
    dz1 = (occupied * gain1 * recip1 * (du1 - sd1 / voxels - xh1 * (sx1 / voxels))).astype(BF16)

    conv_back(dz1, w1_ref)
    rsend_ref[sent:] = eext_ref[bricks:].astype(BF16)
    back1 = (3, lambda n: rsend_ref.at[sent + n], lambda n: ret_ref.at[sent + n], -1)
    start_halo(*back1)
    reduce_step(1, 2)
    conv_weights(0, q1_ref, dz1, root)
    reduce_step(0, 0)
    reduce_step(1, 3)
    reduce_step(0, 1)
    end_halo(*back1)
    ret_base[0] = sent
    back_in = home(eext_ref[:bricks]).reshape(vox, channels)
    gin_ref[...] = ((dv + back_in) * occupied).astype(BF16).reshape(gin_ref.shape)
    for step in (4, 5, 6):
        reduce_step(1, step)
        reduce_step(0, step - 2)
    for step in (5, 6):
        reduce_step(0, step)
    for w in range(2):
        drain_reduce(w)
    for way in (features, raw, back2, back1):
        drain_halo(*way)
    for r in range(4):
        drain_sums(r)


def solution(mesh):
    nx, ny = mesh.shape["gx"], mesh.shape["gy"]

    def body(voxel, w1, w2, gain, shift, grad_out, brick_count, kernel_map, face_send, corner_send):
        bricks, _, channels = voxel.shape
        side, small = face_send.shape[2], corner_send.shape[2]
        sent = 4 * side + 4 * small
        entries = bricks + sent
        field = (bricks, 4, 16, channels)
        rows = bricks * 144
        parts = 2 * nx * (ny // 2)
        chunk = -(-w1.shape[0] * channels // (16 * parts)) * 16
        vmem, smem = pl.BlockSpec(memory_space=pltpu.VMEM), pl.BlockSpec(memory_space=pltpu.SMEM)
        hbm = pl.BlockSpec(memory_space=pl.ANY)
        nz = ny // 2
        taps = w1.shape[0] * channels
        out, gin, dw, norms = pl.pallas_call(
            functools.partial(kernel, nx, ny, side, small),
            out_shape=[
                jax.ShapeDtypeStruct(field, BF16),
                jax.ShapeDtypeStruct(field, BF16),
                jax.ShapeDtypeStruct((2, parts * chunk, channels), BF16),
                jax.ShapeDtypeStruct((4, channels), F32),
            ],
            in_specs=[vmem, hbm, hbm, vmem, vmem, hbm] + [smem] * 4,
            out_specs=[vmem] * 4,
            scratch_shapes=[
                pltpu.VMEM((taps, channels), BF16),
                pltpu.VMEM((taps, channels), BF16),
                pltpu.VMEM(field, BF16),
                pltpu.SemaphoreType.DMA((3,)),
                pltpu.VMEM((3, rows, entries * 16), BF16),
                pltpu.VMEM((3, entries * 16, rows), BF16),
                pltpu.VMEM((entries, 4, 16, channels), F32),
                pltpu.VMEM((entries, 4, 16, channels), BF16),
                pltpu.VMEM((entries, 4, 16, channels), F32),
                pltpu.VMEM((bricks, 4, 16, channels), F32),
                pltpu.VMEM((entries, 4, 16, channels), F32),
                pltpu.VMEM((bricks, 6, 16, 9 * channels), BF16),
                pltpu.VMEM((bricks, 6, 16, 9 * channels), BF16),
                pltpu.VMEM((6, bricks, 9, 16, channels), F32),
                pltpu.VMEM((sent, 4, 16, channels), BF16),
                pltpu.VMEM((sent, 4, 16, channels), F32),
                pltpu.VMEM((2 * sent, 4, 16, channels), BF16),
                pltpu.VMEM((2 * sent, 4, 16, channels), BF16),
                pltpu.VMEM((4, nx, 8, channels), F32),
                pltpu.VMEM((4, ny, 8, channels), F32),
                pltpu.SemaphoreType.DMA((4, sent)),
                pltpu.SemaphoreType.DMA((4, sent)),
                pltpu.SemaphoreType.DMA((4, nx)),
                pltpu.SemaphoreType.DMA((4, nx)),
                pltpu.SemaphoreType.DMA((4, ny)),
                pltpu.SemaphoreType.DMA((4, ny)),
                pltpu.VMEM((2, parts * chunk, channels), BF16),
                pltpu.VMEM((2, parts * chunk // 2, channels), BF16),
                pltpu.VMEM((2, nx, nz * chunk, channels), BF16),
                pltpu.VMEM((2, nx, nz * chunk, channels), BF16),
                pltpu.VMEM((2, nz, chunk, channels), BF16),
                pltpu.VMEM((2, nz, chunk, channels), BF16),
                pltpu.VMEM((2, 2, nx, nz, chunk, channels), BF16),
                pltpu.SemaphoreType.DMA((2, 2)),
                pltpu.SemaphoreType.DMA((2, 2)),
                pltpu.SemaphoreType.DMA((2, 2, nx)),
                pltpu.SemaphoreType.DMA((2, 2, nx)),
                pltpu.SemaphoreType.DMA((2, 2, nz)),
                pltpu.SemaphoreType.DMA((2, 2, nz)),
            ],
            compiler_params=pltpu.CompilerParams(
                collective_id=0, has_side_effects=True, vmem_limit_bytes=56 * 1024 * 1024
            ),
        )(
            voxel.reshape(field), w1.reshape(taps, channels), w2.reshape(taps, channels), gain, shift,
            grad_out.reshape(field), brick_count, kernel_map, face_send, corner_send,
        )
        weight_grads = dw[:, :taps].astype(F32).reshape((2,) + w1.shape)
        return out.reshape(voxel.shape), gin.reshape(voxel.shape), weight_grads, norms

    tiles = P(("gx", "gy"))
    in_specs = (tiles, P(), P(), P(), P(), tiles, tiles, tiles, tiles, tiles)
    return jax.shard_map(
        body, mesh=mesh, in_specs=in_specs, out_specs=(tiles, tiles, P(), P()), check_vma=False
    )
```

```python
import functools

import jax
import jax.numpy as jnp
from jax import lax
from jax.experimental import pallas as pl
from jax.experimental.pallas import tpu as pltpu
from jax.sharding import PartitionSpec as P

MESH = pl.DeviceIdType.MESH
FACES = ((1, 0), (-1, 0), (0, 1), (0, -1))
CORNERS = ((1, 1), (1, -1), (-1, 1), (-1, -1))
epsilon = 1e-05
F32 = jnp.float32
BF16 = jnp.bfloat16


def plane_sources(at):
    s, q, r = at >> 4, (at >> 2) & 3, at & 3
    tens = jnp.where(s >= 6, 2, jnp.where(s >= 3, 1, 0))
    q, r = q + tens - 1, r + s - 3 * tens - 1
    oq = jnp.where(q > 3, 1, jnp.where(q < 0, -1, 0))
    orr = jnp.where(r > 3, 1, jnp.where(r < 0, -1, 0))
    return 3 * (oq + 1) + orr + 1, 4 * (q - 4 * oq) + r - 4 * orr


def sigmoid(values):
    return 1.0 / (1.0 + jnp.exp(-values))


def slope(values):
    sigma = sigmoid(values)
    return sigma * (1.0 + values * (1.0 - sigma))


def dot(a, b, dims=((1,), (0,))):
    return lax.dot_general(a, b, (dims, ((), ())), preferred_element_type=F32)


def kernel(
    nx, ny, side, small,
    voxel_ref, w1_hbm, w2_hbm, gain_ref, shift_ref, grad_hbm, count_ref, map_ref, face_ref, corner_ref,
    out_ref, gin_ref, dw_ref, norms_ref,
    w1_ref, w2_ref, grad_ref, load_sem,
    gather_ref, scatter_ref, mask_ref, fext_ref, zext_ref, zown_ref, eext_ref, q1_ref, q2_ref, d_ref,
    fsend_ref, zsend_ref, rsend_ref, ret_ref, xbuf_ref, ybuf_ref,
    halo_send, halo_recv, x_send, x_recv, y_send, y_recv,
    part_ref, pair_ref, half_ref, cross_ref, quarter_ref, deep_ref, full_ref,
    pair_send, pair_recv, cross_send, cross_recv, deep_send, deep_recv,
):
    i, j = lax.axis_index("gx"), lax.axis_index("gy")
    bricks, _, _, channels = voxel_ref.shape
    entries = fext_ref.shape[0]
    vox = bricks * 64
    items = [(FACES[k], face_ref, k * side + t) for k in range(4) for t in range(side)]
    items += [(CORNERS[k], corner_ref, k * small + t) for k in range(4) for t in range(small)]

    def inside(dx, dy):
        ok = jnp.int32(1)
        if dx > 0:
            ok = ok * (i + 1 < nx).astype(jnp.int32)
        if dx < 0:
            ok = ok * (i > 0).astype(jnp.int32)
        if dy > 0:
            ok = ok * (j + 1 < ny).astype(jnp.int32)
        if dy < 0:
            ok = ok * (j > 0).astype(jnp.int32)
        return ok

    barrier = pltpu.get_barrier_semaphore()
    loads = [
        pltpu.make_async_copy(source, target, load_sem.at[n])
        for n, (source, target) in enumerate([(w1_hbm, w1_ref), (w2_hbm, w2_ref), (grad_hbm, grad_ref)])
    ]
    for load in loads:
        load.start()
    waits = jnp.int32(nx - 1 + ny - 1)
    for k in range(1, nx):
        pl.semaphore_signal(barrier, inc=1, device_id=(lax.rem(i + k, nx), j), device_id_type=MESH)
    for k in range(1, ny):
        pl.semaphore_signal(barrier, inc=1, device_id=(i, lax.rem(j + k, ny)), device_id_type=MESH)
    for dx, dy in CORNERS:
        there = inside(dx, dy)
        waits = waits + there

        @pl.when(there == 1)
        def _():
            pl.semaphore_signal(barrier, inc=1, device_id=(i + dx, j + dy), device_id_type=MESH)

    def halo(round_, n, src, dst, direction):
        dx, dy = direction
        return pltpu.make_async_remote_copy(
            src_ref=src, dst_ref=dst, send_sem=halo_send.at[round_, n], recv_sem=halo_recv.at[round_, n],
            device_id=(i + dx, j + dy), device_id_type=MESH,
        )

    def start_halo(round_, sources, targets, sign):
        for n, ((dx, dy), _, _) in enumerate(items):
            way = (sign * dx, sign * dy)

            @pl.when(inside(*way) == 1)
            def _():
                halo(round_, n, sources(n), targets(n), way).start()

    def end_halo(round_, sources, targets, sign):
        for n, ((dx, dy), _, _) in enumerate(items):
            way = (sign * dx, sign * dy)

            @pl.when(inside(-way[0], -way[1]) == 1)
            def _():
                halo(round_, n, sources(n), targets(n), (-way[0], -way[1])).wait_recv()

    def drain_halo(round_, sources, targets, sign):
        for n, ((dx, dy), _, _) in enumerate(items):
            way = (sign * dx, sign * dy)

            @pl.when(inside(*way) == 1)
            def _():
                halo(round_, n, sources(n), targets(n), way).wait_send()

    def x_copy(r, slot, k, to):
        return pltpu.make_async_remote_copy(
            src_ref=xbuf_ref.at[r, slot], dst_ref=xbuf_ref.at[r, slot], send_sem=x_send.at[r, k],
            recv_sem=x_recv.at[r, k], device_id=(to, j), device_id_type=MESH,
        )

    def y_copy(r, slot, k, to):
        return pltpu.make_async_remote_copy(
            src_ref=ybuf_ref.at[r, slot], dst_ref=ybuf_ref.at[r, slot], send_sem=y_send.at[r, k],
            recv_sem=y_recv.at[r, k], device_id=(i, to), device_id_type=MESH,
        )

    def start_sums(r, rows):
        slab = jnp.concatenate(rows + [jnp.zeros((8 - len(rows), channels), F32)], axis=0)
        xbuf_ref[r, i] = slab
        for k in range(1, nx):
            x_copy(r, i, k, lax.rem(i + k, nx)).start()

    def turn_sums(r):
        for k in range(1, nx):
            x_copy(r, lax.rem(i - k + nx, nx), k, i).wait_recv()
        ybuf_ref[r, j] = jnp.sum(xbuf_ref[r], axis=0)
        for k in range(1, ny):
            y_copy(r, j, k, lax.rem(j + k, ny)).start()

    def end_sums(r, turned=False):
        if not turned:
            turn_sums(r)
        for k in range(1, ny):
            y_copy(r, lax.rem(j - k + ny, ny), k, j).wait_recv()
        return jnp.sum(ybuf_ref[r], axis=0)

    def drain_sums(r):
        for k in range(1, nx):
            x_copy(r, i, k, lax.rem(i + k, nx)).wait_send()
        for k in range(1, ny):
            y_copy(r, j, k, lax.rem(j + k, ny)).wait_send()

    def colsum(values):
        return jnp.sum(values, axis=0, keepdims=True)

    count = count_ref[0]
    entry = lax.broadcasted_iota(jnp.int32, mask_ref.shape, 0)
    mask = jnp.where(entry < count, 1.0, 0.0)
    mask = jnp.where(entry < bricks, mask, 0.0)
    for n, ((dx, dy), _, _) in enumerate(items):
        mask = jnp.where(entry == bricks + n, inside(-dx, -dy).astype(F32), mask)
    mask_ref[...] = mask
    fext_ref[:bricks] = (voxel_ref[...].astype(F32) * mask_ref[:bricks]).astype(BF16)
    for n, (_, list_ref, place) in enumerate(items):
        fsend_ref[n] = voxel_ref[list_ref[place]]
    pl.semaphore_wait(barrier, waits)
    features = (0, lambda n: fsend_ref.at[n], lambda n: fext_ref.at[bricks + n], 1)
    start_halo(*features)

    lane = lax.broadcasted_iota(jnp.int32, (144, entries * 16), 1)
    row = lax.broadcasted_iota(jnp.int32, scatter_ref.shape[1:], 0)
    down, down_place = plane_sources(lax.broadcasted_iota(jnp.int32, (144, 1), 0))
    across = lax.broadcasted_iota(jnp.int32, (1, bricks * 144), 1)
    owner = jnp.zeros_like(across)
    for b in range(1, bricks):
        owner = owner + jnp.where(across >= b * 144, 1, 0)
    along, along_place = plane_sources(across - 144 * owner)
    along = along + 9 * owner
    for o in range(3):
        tall = along_place
        for b in range(bricks):
            target = down_place
            for d in range(9):
                start = 16 * map_ref[b, 9 * o + d]
                target = target + jnp.where(down == d, start, 0)
                tall = tall + jnp.where(along == 9 * b + d, start, 0)
            gather_ref[o, b * 144 : (b + 1) * 144] = jnp.where(lane == target, 1.0, 0.0).astype(BF16)
        scatter_ref[o] = jnp.where(row == tall, 1.0, 0.0).astype(BF16)

    def collect(field, q_ref):
        flat = [field[:, p].reshape(entries * 16, channels) for p in range(4)]
        low = dot(gather_ref[0], flat[3]).astype(BF16)
        mid = dot(gather_ref[1], jnp.concatenate(flat, axis=1)).astype(BF16)
        high = dot(gather_ref[2], flat[0]).astype(BF16)
        planes = [low] + [mid[:, p * channels : (p + 1) * channels] for p in range(4)] + [high]
        for a, plane in enumerate(planes):
            plane = plane.reshape(bricks, 9, 16, channels)
            for s in range(9):
                q_ref[:, a, :, s * channels : (s + 1) * channels] = plane[:, s]

    width = 9 * channels

    def taps(q_ref, a):
        return q_ref[:, a : a + 4].reshape(vox, width)

    def conv(q_ref, w_ref):
        total = dot(taps(q_ref, 0), w_ref[:width])
        for a in (1, 2):
            total = total + dot(taps(q_ref, a), w_ref[a * width : (a + 1) * width])
        return total

    def conv_weights(w, q_ref, grads, scale, planes=(0, 1, 2)):
        for a in planes:
            value = dot(taps(q_ref, a), grads, ((0,), (0,))) * scale
            part_ref[w, a * width : (a + 1) * width] = value.astype(BF16)
        if 2 in planes and part_ref.shape[1] > 3 * width:
            part_ref[w, 3 * width :] = jnp.zeros((part_ref.shape[1] - 3 * width, channels), BF16)

    nz = ny // 2
    mate = lax.rem(j, 2)
    level = j // 2
    chunk = deep_ref.shape[2]
    half = part_ref.shape[1] // 2

    def pair_copy(w, way):
        if way == 0:
            source = part_ref.at[w, pl.ds(pl.multiple_of((1 - mate) * half, 16), half)]
            target = pair_ref.at[w]
        else:
            source = target = full_ref.at[w, mate]
        return pltpu.make_async_remote_copy(
            src_ref=source, dst_ref=target, send_sem=pair_send.at[w, way], recv_sem=pair_recv.at[w, way],
            device_id=(i, j + 1 - 2 * mate), device_id_type=MESH,
        )

    def pair_wait(w, way):
        target = pair_ref.at[w] if way == 0 else full_ref.at[w, 1 - mate]
        pltpu.make_async_remote_copy(
            src_ref=target, dst_ref=target, send_sem=pair_send.at[w, way], recv_sem=pair_recv.at[w, way],
            device_id=(i, j + 1 - 2 * mate), device_id_type=MESH,
        ).wait_recv()

    def cross_copy(w, way, k, receive):
        to = lax.rem(i + k, nx)
        slot = lax.rem(i - k + nx, nx) if receive else i
        target = full_ref.at[w, mate, slot] if way else cross_ref.at[w, slot]
        source = target if way or receive else half_ref.at[w, to]
        return pltpu.make_async_remote_copy(
            src_ref=source, dst_ref=target, send_sem=cross_send.at[w, way, k], recv_sem=cross_recv.at[w, way, k],
            device_id=(to, j), device_id_type=MESH,
        )

    def deep_copy(w, way, k, receive):
        to = lax.rem(level + k, nz)
        slot = lax.rem(level - k + nz, nz) if receive else level
        target = full_ref.at[w, mate, i, slot] if way else deep_ref.at[w, slot]
        source = target if way or receive else quarter_ref.at[w, to]
        return pltpu.make_async_remote_copy(
            src_ref=source, dst_ref=target, send_sem=deep_send.at[w, way, k], recv_sem=deep_recv.at[w, way, k],
            device_id=(i, 2 * to + mate), device_id_type=MESH,
        )

    def reduce_step(w, step):
        if step == 0:
            pair_copy(w, 0).start()
        if step == 1:
            pair_wait(w, 0)
            own = part_ref[w, pl.ds(pl.multiple_of(mate * half, 16), half)]
            value = own.astype(F32) + pair_ref[w].astype(F32)
            half_ref[w] = value.astype(BF16).reshape(half_ref.shape[1:])
            for k in range(1, nx):
                cross_copy(w, 0, k, False).start()
            cross_ref[w, i] = half_ref[w, i]
        if step == 2:
            for k in range(1, nx):
                cross_copy(w, 0, k, True).wait_recv()
            value = jnp.sum(cross_ref[w].astype(F32), axis=0)
            quarter_ref[w] = value.astype(BF16).reshape(quarter_ref.shape[1:])
            for k in range(1, nz):
                deep_copy(w, 0, k, False).start()
            deep_ref[w, level] = quarter_ref[w, level]
        if step == 3:
            for k in range(1, nz):
                deep_copy(w, 0, k, True).wait_recv()
            full_ref[w, mate, i, level] = jnp.sum(deep_ref[w].astype(F32), axis=0).astype(BF16)
            for k in range(1, nz):
                deep_copy(w, 1, k, False).start()
        if step == 4:
            for k in range(1, nz):
                deep_copy(w, 1, k, True).wait_recv()
            for k in range(1, nx):
                cross_copy(w, 1, k, False).start()
        if step == 5:
            for k in range(1, nx):
                cross_copy(w, 1, k, True).wait_recv()
            pair_copy(w, 1).start()
        if step == 6:
            pair_wait(w, 1)
            dw_ref[w] = full_ref[w].reshape(part_ref.shape[1:])[: 3 * width]

    def drain_reduce(w):
        for way in range(2):
            pair_copy(w, way).wait_send()
            for k in range(1, nx):
                cross_copy(w, way, k, False).wait_send()
            for k in range(1, nz):
                deep_copy(w, way, k, False).wait_send()

    def conv_back(grads, w_ref):
        parts = [
            dot(grads, w_ref[a * width : (a + 1) * width], ((1,), (1,))).reshape(bricks, 4, 16, width)
            for a in range(3)
        ]
        for a6 in range(6):
            piece = None
            for a in range(3):
                if 0 <= a6 - a < 4:
                    term = parts[a][:, a6 - a]
                    piece = term if piece is None else piece + term
            for s in range(9):
                d_ref[a6, :, s] = piece[:, :, s * channels : (s + 1) * channels]

        def spread(o, planes):
            value = [d_ref[a6].reshape(bricks * 144, channels) for a6 in planes]
            value = value[0] if len(value) == 1 else jnp.concatenate(value, axis=1)
            upper = value.astype(BF16)
            lower = (value - upper.astype(F32)).astype(BF16)
            return dot(scatter_ref[o], upper) + dot(scatter_ref[o], lower)

        mid = spread(1, (1, 2, 3, 4))
        low, high = spread(0, (0,)), spread(2, (5,))
        for p in range(4):
            value = mid[:, p * channels : (p + 1) * channels]
            if p == 3:
                value = value + low
            if p == 0:
                value = value + high
            eext_ref[:, p] = value.reshape(entries, 16, channels)

    def home(values):
        brick = lax.broadcasted_iota(jnp.int32, values.shape, 0)
        for n, ((dx, dy), list_ref, place) in enumerate(items):
            chosen = jnp.where(inside(dx, dy) == 1, list_ref[place], -1)
            values = values + jnp.where(brick == chosen, ret_ref[ret_base[0] + n].astype(F32)[None], 0.0)
        return values

    ret_base = [0]
    sent = len(items)

    end_halo(*features)
    fext_ref[bricks:] = jnp.where(mask_ref[bricks:] > 0.0, fext_ref[bricks:].astype(F32), 0.0).astype(BF16)
    collect(fext_ref, q1_ref)
    loads[0].wait()
    z1 = conv(q1_ref, w1_ref)
    zown_ref[...] = z1.reshape(bricks, 4, 16, channels)
    for n, (_, list_ref, place) in enumerate(items):
        zsend_ref[n] = zown_ref[list_ref[place]]
    raw = (1, lambda n: zsend_ref.at[n], lambda n: zext_ref.at[bricks + n], 1)
    occupied = mask_ref[:bricks].reshape(vox, channels)
    weighted = jnp.zeros((1, channels), F32) + 64.0 * count.astype(F32)
    start_sums(0, [colsum(z1 * occupied), colsum(z1 * z1 * occupied), weighted])
    start_halo(*raw)
    totals = end_sums(0)
    voxels = totals[2:3]
    mean1 = totals[0:1] / voxels
    recip1 = lax.rsqrt(totals[1:2] / voxels - mean1 * mean1 + epsilon)
    end_halo(*raw)

    gain1, gain2 = gain_ref[0:1], gain_ref[1:2]
    shift1, shift2 = shift_ref[0:1], shift_ref[1:2]
    wide = mask_ref[...].reshape(entries * 64, channels)
    zext_ref[:bricks] = zown_ref[...]
    zall = jnp.where(wide > 0.0, zext_ref[...].reshape(entries * 64, channels), 0.0)
    xh1 = (zall - mean1) * recip1
    zext_ref[...] = xh1.reshape(zext_ref.shape)
    u1 = gain1 * xh1 + shift1
    a1 = (u1 * sigmoid(u1) * wide).astype(BF16)
    collect(a1.reshape(entries, 4, 16, channels), q2_ref)
    loads[1].wait()
    z2 = conv(q2_ref, w2_ref)
    start_sums(1, [colsum(z2 * occupied), colsum(z2 * z2 * occupied)])
    totals = end_sums(1)
    mean2 = totals[0:1] / voxels
    recip2 = lax.rsqrt(totals[1:2] / voxels - mean2 * mean2 + epsilon)
    xh2 = (z2 - mean2) * recip2
    feats = fext_ref[:bricks].astype(F32).reshape(vox, channels)
    pre = gain2 * xh2 + shift2 + feats
    loads[2].wait()
    dv = grad_ref[...].astype(F32).reshape(vox, channels) * occupied * slope(pre)
    start_sums(2, [colsum(dv), colsum(dv * xh2)])
    out_ref[...] = (pre * sigmoid(pre) * occupied).astype(BF16).reshape(out_ref.shape)
    totals = end_sums(2)
    sd2, sx2 = totals[0:1], totals[1:2]
    dz2 = (occupied * gain2 * recip2 * (dv - sd2 / voxels - xh2 * (sx2 / voxels))).astype(BF16)
    root = lax.rsqrt(voxels)

    conv_back(dz2, w2_ref)
    rsend_ref[:sent] = eext_ref[bricks:].astype(BF16)
    back2 = (2, lambda n: rsend_ref.at[n], lambda n: ret_ref.at[n], -1)
    start_halo(*back2)
    xh1 = zext_ref[...].reshape(entries * 64, channels)
    part = eext_ref[...].reshape(entries * 64, channels) * wide * slope(gain1 * xh1 + shift1)
    start_sums(3, [colsum(part), colsum(part * xh1)])
    conv_weights(1, q2_ref, dz2, root, (0,))
    turn_sums(3)
    conv_weights(1, q2_ref, dz2, root, (1, 2))
    reduce_step(1, 0)
    totals = end_sums(3, True)
    reduce_step(1, 1)
    sd1, sx1 = totals[0:1], totals[1:2]
    norms_ref[...] = jnp.concatenate([sx1, sd1, sx2, sd2], axis=0) * root
    end_halo(*back2)
    da1 = home(eext_ref[:bricks]).reshape(vox, channels)
    xh1 = zext_ref[:bricks].reshape(vox, channels)
    du1 = da1 * occupied * slope(gain1 * xh1 + shift1)
    dz1 = (occupied * gain1 * recip1 * (du1 - sd1 / voxels - xh1 * (sx1 / voxels))).astype(BF16)

    conv_weights(0, q1_ref, dz1, root)
    reduce_step(0, 0)
    reduce_step(1, 2)
    reduce_step(0, 1)
    conv_back(dz1, w1_ref)
    rsend_ref[sent:] = eext_ref[bricks:].astype(BF16)
    back1 = (3, lambda n: rsend_ref.at[sent + n], lambda n: ret_ref.at[sent + n], -1)
    start_halo(*back1)
    reduce_step(1, 3)
    reduce_step(0, 2)
    reduce_step(1, 4)
    end_halo(*back1)
    ret_base[0] = sent
    back_in = home(eext_ref[:bricks]).reshape(vox, channels)
    gin_ref[...] = ((dv + back_in) * occupied).astype(BF16).reshape(gin_ref.shape)
    for step in (3, 4):
        reduce_step(0, step)
        reduce_step(1, step + 2)
    for step in (5, 6):
        reduce_step(0, step)
    for w in range(2):
        drain_reduce(w)
    for way in (features, raw, back2, back1):
        drain_halo(*way)
    for r in range(4):
        drain_sums(r)


def solution(mesh):
    nx, ny = mesh.shape["gx"], mesh.shape["gy"]

    def body(voxel, w1, w2, gain, shift, grad_out, brick_count, kernel_map, face_send, corner_send):
        bricks, _, channels = voxel.shape
        side, small = face_send.shape[2], corner_send.shape[2]
        sent = 4 * side + 4 * small
        entries = bricks + sent
        field = (bricks, 4, 16, channels)
        rows = bricks * 144
        parts = 2 * nx * (ny // 2)
        chunk = -(-w1.shape[0] * channels // (16 * parts)) * 16
        vmem, smem = pl.BlockSpec(memory_space=pltpu.VMEM), pl.BlockSpec(memory_space=pltpu.SMEM)
        hbm = pl.BlockSpec(memory_space=pl.ANY)
        nz = ny // 2
        taps = w1.shape[0] * channels
        out, gin, dw, norms = pl.pallas_call(
            functools.partial(kernel, nx, ny, side, small),
            out_shape=[
                jax.ShapeDtypeStruct(field, BF16),
                jax.ShapeDtypeStruct(field, BF16),
                jax.ShapeDtypeStruct((2, taps, channels), BF16),
                jax.ShapeDtypeStruct((4, channels), F32),
            ],
            in_specs=[vmem, hbm, hbm, vmem, vmem, hbm] + [smem] * 4,
            out_specs=[vmem] * 4,
            scratch_shapes=[
                pltpu.VMEM((taps, channels), BF16),
                pltpu.VMEM((taps, channels), BF16),
                pltpu.VMEM(field, BF16),
                pltpu.SemaphoreType.DMA((3,)),
                pltpu.VMEM((3, rows, entries * 16), BF16),
                pltpu.VMEM((3, entries * 16, rows), BF16),
                pltpu.VMEM((entries, 4, 16, channels), F32),
                pltpu.VMEM((entries, 4, 16, channels), BF16),
                pltpu.VMEM((entries, 4, 16, channels), F32),
                pltpu.VMEM((bricks, 4, 16, channels), F32),
                pltpu.VMEM((entries, 4, 16, channels), F32),
                pltpu.VMEM((bricks, 6, 16, 9 * channels), BF16),
                pltpu.VMEM((bricks, 6, 16, 9 * channels), BF16),
                pltpu.VMEM((6, bricks, 9, 16, channels), F32),
                pltpu.VMEM((sent, 4, 16, channels), BF16),
                pltpu.VMEM((sent, 4, 16, channels), F32),
                pltpu.VMEM((2 * sent, 4, 16, channels), BF16),
                pltpu.VMEM((2 * sent, 4, 16, channels), BF16),
                pltpu.VMEM((4, nx, 8, channels), F32),
                pltpu.VMEM((4, ny, 8, channels), F32),
                pltpu.SemaphoreType.DMA((4, sent)),
                pltpu.SemaphoreType.DMA((4, sent)),
                pltpu.SemaphoreType.DMA((4, nx)),
                pltpu.SemaphoreType.DMA((4, nx)),
                pltpu.SemaphoreType.DMA((4, ny)),
                pltpu.SemaphoreType.DMA((4, ny)),
                pltpu.VMEM((2, parts * chunk, channels), BF16),
                pltpu.VMEM((2, parts * chunk // 2, channels), BF16),
                pltpu.VMEM((2, nx, nz * chunk, channels), BF16),
                pltpu.VMEM((2, nx, nz * chunk, channels), BF16),
                pltpu.VMEM((2, nz, chunk, channels), BF16),
                pltpu.VMEM((2, nz, chunk, channels), BF16),
                pltpu.VMEM((2, 2, nx, nz, chunk, channels), BF16),
                pltpu.SemaphoreType.DMA((2, 2)),
                pltpu.SemaphoreType.DMA((2, 2)),
                pltpu.SemaphoreType.DMA((2, 2, nx)),
                pltpu.SemaphoreType.DMA((2, 2, nx)),
                pltpu.SemaphoreType.DMA((2, 2, nz)),
                pltpu.SemaphoreType.DMA((2, 2, nz)),
            ],
            compiler_params=pltpu.CompilerParams(
                collective_id=0, has_side_effects=True, vmem_limit_bytes=56 * 1024 * 1024
            ),
        )(
            voxel.reshape(field), w1.reshape(taps, channels), w2.reshape(taps, channels), gain, shift,
            grad_out.reshape(field), brick_count, kernel_map, face_send.reshape(-1), corner_send.reshape(-1),
        )
        weight_grads = dw.astype(F32).reshape((2,) + w1.shape)
        return out.reshape(voxel.shape), gin.reshape(voxel.shape), weight_grads, norms

    tiles = P(("gx", "gy"))
    in_specs = (tiles, P(), P(), P(), P(), tiles, tiles, tiles, tiles, tiles)
    return jax.shard_map(
        body, mesh=mesh, in_specs=in_specs, out_specs=(tiles, tiles, P(), P()), check_vma=False
    )
```
